32 devices in a mesh: dp: 4 (over z), chan: 2 (over y), seq: 4 (over x, core).
Axes of the slice: x: 2, y: 2, z: 4, core: 2. Of those that a mesh axis runs over, the one named last changes fastest.
Arguments:
- tokens: bfloat16 [4, 4096, 768], P('dp', 'seq', 'chan'), may hold values from -6 to 6
- chan_in: bfloat16 [12, 64, 64], replicated, may hold values from -0.75 to 0.75
- chan_out: bfloat16 [64, 12, 12], replicated, may hold values from -1.75 to 1.75
- seq_in: bfloat16 [1024, 1024], replicated, may hold values from -0.1875 to 0.1875
- seq_out: bfloat16 [4, 4], replicated, may hold values from -3 to 3
- head_grad: bfloat16 [4, 4096, 768], P('dp', 'seq', 'chan'), may hold values from -6 to 6
- masked: int32 [4, 4096], P('dp', 'seq'), may hold values 0 or 1
Outputs:
- x_grad: bfloat16 [4, 4096, 768], P('dp', 'seq', 'chan')
- chan_in_grad: float32 [12, 64, 64], replicated
- chan_out_grad: float32 [64, 12, 12], replicated
- seq_in_grad: float32 [1024, 1024], P('seq')
- seq_out_grad: float32 [4, 4], replicated
The draws below stay inside these ranges and needn't reach their ends.
All inputs are finite; a program needn't handle non-finite values. No bound on the sum of `masked` on one device may be relied on, other than what follows from the above.
Results may differ from the reference program's by a relative error of at most 0.0083.
Values may be sent and summed in bfloat16 or wider, within the bound.
No kernel may reach another device: no remote copies, remote signals or barrier semaphores. Data moves between devices by JAX's collectives and lax.ppermute only.
A program may use at most 64 MiB of HBM per device.

```python
import jax
import jax.numpy as jnp
from jax import lax

BLOCK = 64
NBLK = 12
D = 768
TOK_DEV = 1024
SEQ_LEN = 4096
SEQ_ALL = 4
N_SEQ = 4


def plant(result, own_key, smallest, top_value):
    index_at = [jax.random.randint(jax.random.fold_in(own_key, axis), (), 0, length) for axis, length in enumerate(result.shape)]
    widest = result.shape.index(max(result.shape))
    beside = index_at[:widest] + [(index_at[widest] + 1) % result.shape[widest]] + index_at[widest + 1:]
    return result.at[tuple(index_at)].set(smallest).at[tuple(beside)].set(top_value)


def shard_levels(rng, dims, cuts, low, top_value):
    level, own = 1.0, jax.random.fold_in(rng, 6)
    for axis_at, parts in cuts:
        steps = jnp.exp(jax.random.uniform(jax.random.fold_in(own, axis_at), (parts,), jnp.float32, low / len(cuts), top_value / len(cuts)))
        level = level * jnp.repeat(steps, dims[axis_at] // parts).reshape([-1 if axis == axis_at else 1 for axis in range(len(dims))])
    return level


def scatter_about(stream_key, dims, spread, bound, split=(), kind=jnp.bfloat16):
    entries = jax.random.normal(stream_key, dims, jnp.float32) * spread
    if len(split) > 0:
        entries = shard_levels(stream_key, dims, split, -0.22, 0.18) * entries
    return jnp.clip(entries, min=-bound, max=bound).astype(kind)


def setup_inputs(seed: int = 0) -> dict:
    arg_keys = jax.random.split(jax.random.key(seed), 8)
    tokens = scatter_about(arg_keys[0], (SEQ_ALL, SEQ_LEN, D), 1.0, 6.0, ((0, 4), (1, 4), (2, 2)))
    chan_in = scatter_about(arg_keys[1], (NBLK, BLOCK, BLOCK), BLOCK ** -0.5, 0.75)
    chan_out = scatter_about(arg_keys[2], (BLOCK, NBLK, NBLK), NBLK ** -0.5, 1.75)
    seq_in = scatter_about(arg_keys[3], (TOK_DEV, TOK_DEV), TOK_DEV ** -0.5, 0.1875)
    seq_out = scatter_about(arg_keys[4], (N_SEQ, N_SEQ), N_SEQ ** -0.5, 3.0)
    head_grad = scatter_about(arg_keys[5], (SEQ_ALL, SEQ_LEN, D), 1.0, 6.0, ((0, 4), (1, 4), (2, 2)))
    masked = plant((jax.random.randint(arg_keys[6], (SEQ_ALL, SEQ_LEN), 0, 100) < 15).astype(jnp.int32), jax.random.fold_in(arg_keys[6], 1), 0, 1)
    return dict(tokens=tokens, chan_in=chan_in, chan_out=chan_out, seq_in=seq_in, seq_out=seq_out, head_grad=head_grad, masked=masked)


def silu_grad(values):
    sig = jax.nn.sigmoid(values)
    return sig * (1.0 + values * (1.0 - sig))

def reference(tokens, chan_in, chan_out, seq_in, seq_out, head_grad, masked):
    in_full = chan_in.astype(jnp.float32)
    out_full = chan_out.astype(jnp.float32)
    seq_first = seq_in.astype(jnp.float32)
    seq_second = seq_out.astype(jnp.float32)

    def one_sequence(totals, inputs):
        features, head_rows, mask_rows = inputs
        feat_f = features.astype(jnp.float32).reshape(SEQ_LEN, NBLK, BLOCK)
        first_mix = jnp.einsum('pbk,bki->pib', feat_f, in_full).astype(jnp.bfloat16)
        first_f = first_mix.astype(jnp.float32)
        channel_mix = jnp.einsum('pib,ibe->pie', first_f, out_full).astype(jnp.bfloat16).reshape(SEQ_LEN, D)
        mix_f = channel_mix.astype(jnp.float32)
        mix_blocks = mix_f.reshape(N_SEQ, TOK_DEV, D)
        row_mix = jnp.einsum('atc,tr->arc', mix_blocks, seq_first).astype(jnp.bfloat16)
        row_f = row_mix.astype(jnp.float32)
        seq_mix = jnp.einsum('atc,ab->tbc', row_f, seq_second).reshape(SEQ_LEN, D)
        upstream = mask_rows[:, None].astype(jnp.float32) * head_rows.astype(jnp.float32)
        gated_grad = (upstream * jax.nn.silu(mix_f)).astype(jnp.bfloat16)
        gate_grad = upstream * seq_mix * silu_grad(mix_f)
        gated_f = gated_grad.astype(jnp.float32).reshape(TOK_DEV, N_SEQ, D)
        row_grad = jnp.einsum('ab,tbc->atc', seq_second, gated_f).astype(jnp.bfloat16)
        second_acc = jnp.einsum('atc,tbc->ab', row_f, gated_f)
        row_grad_f = row_grad.astype(jnp.float32)
        seq_part = jnp.einsum('tr,arc->atc', seq_first, row_grad_f).reshape(SEQ_LEN, D)
        mix_grad = (gate_grad + seq_part).astype(jnp.bfloat16)
        first_acc = jnp.einsum('atc,arc->tr', mix_blocks, row_grad_f)
        mix_grad_f = mix_grad.astype(jnp.float32).reshape(SEQ_LEN, BLOCK, NBLK)
        first_grad = jnp.einsum('ibe,pie->pib', out_full, mix_grad_f).astype(jnp.bfloat16)
        out_acc = jnp.einsum('pib,pie->ibe', first_f, mix_grad_f)
        first_grad_f = first_grad.astype(jnp.float32)
        input_grad = jnp.einsum('bki,pib->pbk', in_full, first_grad_f).reshape(SEQ_LEN, D).astype(jnp.bfloat16)
        in_acc = jnp.einsum('pbk,pib->bki', feat_f, first_grad_f)
        new_totals = (totals[0] + in_acc, totals[1] + out_acc, totals[2] + first_acc, totals[3] + second_acc)
        return (new_totals, input_grad)
    start = (jnp.zeros((NBLK, BLOCK, BLOCK), jnp.float32), jnp.zeros((BLOCK, NBLK, NBLK), jnp.float32), jnp.zeros((TOK_DEV, TOK_DEV), jnp.float32), jnp.zeros((N_SEQ, N_SEQ), jnp.float32))
    totals, x_grad = lax.scan(one_sequence, start, (tokens, head_grad, masked))
    return (x_grad, totals[0], totals[1], totals[2], totals[3])
```

```python
import functools

import jax
import jax.numpy as jnp
from jax import lax
from jax.experimental import pallas as pl
from jax.experimental.pallas import tpu as pltpu
from jax.sharding import PartitionSpec as P

F32 = jnp.float32
BF16 = jnp.bfloat16
VMEM_LIMIT = 48 * 1024 * 1024
PACK_LANES = 128


def dot(lhs, rhs, lhs_dim=1, rhs_dim=0):
    return lax.dot_general(
        lhs, rhs, (((lhs_dim,), (rhs_dim,)), ((), ())), preferred_element_type=F32
    )


def dot_exact(lhs, rhs, lhs_dim=1, rhs_dim=0):
    return lax.dot_general(
        lhs,
        rhs,
        (((lhs_dim,), (rhs_dim,)), ((), ())),
        precision=lax.Precision.HIGHEST,
        preferred_element_type=F32,
    )


def rows_of(shape):
    return lax.broadcasted_iota(jnp.int32, shape, 0)


def columns_of(shape):
    return lax.broadcasted_iota(jnp.int32, shape, 1)


def call(body, outs, args, scratch=(), flops=0, name=None):
    nbytes = sum(a.size * a.dtype.itemsize for a in list(args) + list(outs))
    return pl.pallas_call(
        body,
        out_shape=tuple(outs),
        in_specs=[pl.BlockSpec(memory_space=pltpu.VMEM)] * len(args),
        out_specs=tuple([pl.BlockSpec(memory_space=pltpu.VMEM)] * len(outs)),
        scratch_shapes=list(scratch),
        compiler_params=pltpu.CompilerParams(vmem_limit_bytes=VMEM_LIMIT),
        cost_estimate=pl.CostEstimate(flops=flops, bytes_accessed=nbytes, transcendentals=0),
        name=name,
    )(*args)


def struct(shape, dtype=BF16):
    return jax.ShapeDtypeStruct(shape, dtype)


class Sizes:
    def __init__(self, tokens, chan_in, seq_count):
        self.positions, self.width = tokens.shape
        self.blocks, self.block = chan_in.shape[0], chan_in.shape[1]
        self.my_blocks = self.blocks // 2
        self.my_lanes = self.block // 2
        self.half = self.positions // 2
        self.part = self.my_blocks * self.my_lanes
        self.seq = seq_count
        self.group = self.positions // seq_count
        self.step = min(64, self.group)
        self.chunk = self.step * seq_count
        self.chunks = self.positions // self.chunk
        self.direct = seq_count == 4


def in_matrices(z, blocks, lane_base):
    shape = (z.width, 2 * z.part)
    column = columns_of((z.block, 2 * z.part))
    pick = rows_of((z.block, 2 * z.part)) == lane_base + (column & (z.my_lanes - 1))
    spread = dot(blocks, pick.astype(BF16))
    row, column = rows_of(shape), columns_of(shape)
    left = column < z.part
    place = jnp.where(left, column, column - z.part)
    same = (row // z.block) == (place // z.my_lanes)
    lower = jnp.where(same & left, spread, 0.0).astype(BF16)
    upper = jnp.where(same & jnp.logical_not(left), spread, 0.0).astype(BF16)
    return lower, upper


def lane_masks(z):
    shape = (z.width, 2 * z.part)
    row, column = rows_of(shape), columns_of(shape)
    left = column < z.part
    place = jnp.where(left, column, column - z.part)
    same = (row // z.block) == (place // z.my_lanes)
    return same & left, same & jnp.logical_not(left)


def lane_of_channel(z, shape, axis):
    index = lax.broadcasted_iota(jnp.int32, shape, axis)
    lane = (index * 5462) >> 16
    return lane, index - z.blocks * lane


def out_mask(z):
    shape = (z.blocks * z.my_lanes, z.width)
    lane, _ = lane_of_channel(z, shape, 1)
    return (rows_of(shape) & (z.my_lanes - 1)) == lane


def out_matrix(z, factors):
    shape = (z.blocks, z.width)
    _, entry = lane_of_channel(z, shape, 1)
    spread = dot(factors, (rows_of(shape) == entry).astype(BF16))
    return jnp.where(out_mask(z), spread, 0.0).astype(BF16)


def position_masks(z):
    shape = (z.chunk, z.chunk)
    row, column = rows_of(shape), columns_of(shape)
    same = (row & (z.step - 1)) == (column // z.seq)
    blocks = (z.chunk, z.seq)
    of_a = (rows_of(blocks) // z.step) == columns_of(blocks)
    turned = (z.seq, z.chunk)
    of_a2 = (columns_of(turned) & (z.seq - 1)) == rows_of(turned)
    return same, of_a, of_a2


def position_matrix(z, factor):
    same, of_a, of_a2 = position_masks(z)
    by_row = dot(of_a.astype(BF16), factor).astype(BF16)
    return jnp.where(same, dot(by_row, of_a2.astype(BF16)), 0.0).astype(BF16)


def fill_padded(z, pad_ref, rows):
    zeros = jnp.zeros((z.part, z.width), BF16)
    pad_ref[0 : z.part, :] = zeros
    pad_ref[z.part : 2 * z.part, :] = rows
    pad_ref[2 * z.part : 3 * z.part, :] = zeros


def split_blocks(z, full_ref, refs):
    if not z.direct:
        refs[0][...] = full_ref[...]
        return
    mine = lax.axis_index("seq")
    for step, ref in enumerate(refs):
        ref[...] = full_ref[mine ^ step]


def join_blocks(z, refs, full_ref):
    if not z.direct:
        full_ref[...] = refs[0][...]
        return
    mine = lax.axis_index("seq")
    for step, ref in enumerate(refs):
        full_ref[mine ^ step] = ref[...]


def block_outs(z):
    if not z.direct:
        return [struct((z.seq, z.group, z.width))]
    return [struct((z.group, z.width))] * z.seq


def swap(value, axis, step):
    size = lax.axis_size(axis)
    return lax.ppermute(value, axis, [(i, i ^ step) for i in range(size)])


def exchange_blocks(z, blocks):
    if not z.direct:
        return [lax.all_to_all(blocks[0], "seq", split_axis=0, concat_axis=0, tiled=True)]
    return [blocks[0]] + [swap(blocks[step], "seq", step) for step in range(1, z.seq)]


def first_mix_kernel(z, x_ref, in_ref, own_ref, other_ref):
    chan = lax.axis_index("chan")
    blocks = in_ref[pl.ds(chan * z.my_blocks, z.my_blocks)].reshape(z.width, z.block)
    low, high = x_ref[: z.half, :], x_ref[z.half :, :]
    for base, ref in ((1 - chan, other_ref), (chan, own_ref)):
        lower, upper = in_matrices(z, blocks, base * z.my_lanes)
        ref[...] = (dot(low, lower) + dot(high, upper)).astype(BF16)


def prepare_kernel(z, head_ref, mask_ref, seq_ref, out_ref, up_ref, turn_ref, dense_ref):
    lines = jnp.broadcast_to(mask_ref[...].astype(F32), (16, z.positions)).astype(BF16)
    ones = jnp.full((16, z.width), 1.0 / 16.0, BF16)
    mask = dot(lines, ones, 0, 0)
    up_ref[...] = (mask * head_ref[...].astype(F32)).astype(BF16)
    turn_ref[...] = jnp.transpose(seq_ref[...])
    dense_ref[...] = out_matrix(z, out_ref[...])


def channel_mix_kernel(z, own_ref, got_ref, dense_ref, up_ref, so_ref, *rest):
    mix_ref, gated_ref = rest[:2]
    refs, (pad_ref, rows_ref) = rest[2:-2], rest[-2:]
    chan = lax.axis_index("chan")
    low = high = None
    for base, ref in ((chan, own_ref), (1 - chan, got_ref)):
        start = pl.multiple_of(base * z.part, z.part)
        fill_padded(z, pad_ref, dense_ref[pl.ds(start, z.part), :])
        first = dot(ref[...], pad_ref[z.part :, :])
        second = dot(ref[...], pad_ref[: 2 * z.part, :])
        low = first if low is None else low + first
        high = second if high is None else high + second
    for at, values in ((0, low), (z.half, high)):
        rounded = values.astype(BF16)
        mix_ref[at : at + z.half, :] = rounded
        mixed = rounded.astype(F32)
        upstream = up_ref[at : at + z.half, :].astype(F32)
        gated_ref[at : at + z.half, :] = (upstream * (mixed * jax.nn.sigmoid(mixed))).astype(BF16)
    matrix = position_matrix(z, so_ref[...])
    for j in range(z.chunks):
        out = dot(matrix, gated_ref[j * z.chunk : (j + 1) * z.chunk, :]).astype(BF16)
        rows_ref[:, j * z.step : (j + 1) * z.step, :] = out.reshape(z.seq, z.step, z.width)
    split_blocks(z, rows_ref, refs)


def row_mix_kernel(z, turn_ref, mix_ref, *rest):
    refs, rows_ref = rest[:-1], rest[-1]
    out = dot(turn_ref[...], mix_ref[...]).astype(BF16)
    rows_ref[...] = out.reshape(z.seq, z.group, z.width)
    split_blocks(z, rows_ref, refs)


def gate_kernel(z, mix_ref, up_ref, gate_ref):
    mixed = mix_ref[...].astype(F32)
    sig = jax.nn.sigmoid(mixed)
    gate_ref[...] = up_ref[...].astype(F32) * (sig * (1.0 + mixed * (1.0 - sig)))


def seq_grad_kernel(z, count, *rest):
    seq_ref, mix_ref = rest[:2]
    refs = rest[2 : 2 + count]
    part_ref = rest[2 + count]
    outs, rows_ref = rest[3 + count : -1], rest[-1]
    join_blocks(z, refs, rows_ref)
    rows = rows_ref[...].reshape(z.positions, z.width)
    part_ref[...] = dot(seq_ref[...], rows)
    if not z.direct:
        outs[0][...] = dot(mix_ref[...], rows, 1, 1)
        return
    mine = lax.axis_index("seq")
    core = mine & 1
    for x in range(2):
        for keep, out in ((core, outs[0]), (1 - core, outs[1])):
            start = pl.multiple_of((2 * x + keep) * z.group, z.group)
            out[x] = dot(mix_ref[pl.ds(start, z.group), :], rows, 1, 1).astype(BF16)


def mix_grad_kernel(z, count, *rest):
    gate_ref, part_ref, dense_ref, so_ref = rest[:4]
    refs = rest[4 : 4 + count]
    mixg_ref, own_ref, other_ref, spread_ref, pad_ref = rest[4 + count :]
    join_blocks(z, refs, spread_ref)
    matrix = position_matrix(z, so_ref[...])
    for j in range(z.chunks):
        rows = spread_ref[:, j * z.step : (j + 1) * z.step, :].reshape(z.chunk, z.width)
        seq_mix = dot(matrix, rows, 0, 0)
        at = slice(j * z.chunk, (j + 1) * z.chunk)
        mixg_ref[at, :] = (gate_ref[at, :] * seq_mix + part_ref[at, :]).astype(BF16)
    chan = lax.axis_index("chan")
    low, high = mixg_ref[: z.half, :], mixg_ref[z.half :, :]
    for base, ref in ((1 - chan, other_ref), (chan, own_ref)):
        start = pl.multiple_of(base * z.part, z.part)
        fill_padded(z, pad_ref, dense_ref[pl.ds(start, z.part), :])
        total = dot(low, pad_ref[z.part :, :], 1, 1) + dot(high, pad_ref[: 2 * z.part, :], 1, 1)
        ref[...] = total.astype(BF16)


def out_grad_kernel(z, count, *rest):
    own_ref, got_ref, mixg_ref, gated_ref = rest[:4]
    refs = rest[4 : 4 + count]
    out_ref, second_ref, spread_ref, full_ref = rest[4 + count :]
    join_blocks(z, refs, spread_ref)
    chan = lax.axis_index("chan")
    low, high = mixg_ref[: z.half, :], mixg_ref[z.half :, :]
    for base, ref in ((chan, own_ref), (1 - chan, got_ref)):
        first = dot(ref[...], low, 0, 0)[: z.part, :]
        second = dot(ref[...], high, 0, 0)[z.part :, :]
        full_ref[pl.ds(pl.multiple_of(base * z.part, z.part), z.part), :] = first + second
    kept = jnp.where(out_mask(z), full_ref[...], 0.0)
    shape = (z.width, PACK_LANES)
    _, entry = lane_of_channel(z, shape, 0)
    out_ref[...] = dot_exact(kept, (columns_of(shape) == z.block + entry).astype(F32))
    same, of_a, of_a2 = position_masks(z)
    total = jnp.zeros((z.chunk, z.chunk), F32)
    for j in range(z.chunks):
        rows = spread_ref[:, j * z.step : (j + 1) * z.step, :].reshape(z.chunk, z.width)
        total = total + dot(rows, gated_ref[j * z.chunk : (j + 1) * z.chunk, :], 1, 1)
    total = jnp.where(same, total, 0.0)
    shape = (z.chunk, PACK_LANES)
    to_a2 = ((rows_of(shape) & (z.seq - 1)) == columns_of(shape)).astype(F32)
    tall = (max(16, z.seq), z.chunk)
    to_a = ((columns_of(tall) // z.step) == rows_of(tall)).astype(F32)
    second_ref[...] = dot_exact(to_a, dot_exact(total, to_a2))


def in_grad_kernel(z, x_ref, in_ref, own_ref, got_ref, out_ref, second_ref, xg_ref, pack_ref):
    chan = lax.axis_index("chan")
    blocks = in_ref[pl.ds(chan * z.my_blocks, z.my_blocks)].reshape(z.width, z.block)
    low, high = x_ref[: z.half, :], x_ref[z.half :, :]
    left, right = lane_masks(z)
    shape = (2 * z.part, PACK_LANES)
    xg_low = xg_high = None
    pack = out_ref[...]
    for base, ref in ((chan, own_ref), (1 - chan, got_ref)):
        grad = ref[...]
        lower, upper = in_matrices(z, blocks, base * z.my_lanes)
        first, second = dot(grad, lower, 1, 1), dot(grad, upper, 1, 1)
        xg_low = first if xg_low is None else xg_low + first
        xg_high = second if xg_high is None else xg_high + second
        products = jnp.where(left, dot(low, grad, 0, 0), jnp.where(right, dot(high, grad, 0, 0), 0.0))
        lane = base * z.my_lanes + (rows_of(shape) & (z.my_lanes - 1))
        pack = pack + dot_exact(products, (columns_of(shape) == lane).astype(F32))
    xg_ref[: z.half, :] = xg_low.astype(BF16)
    xg_ref[z.half :, :] = xg_high.astype(BF16)
    pack_ref[: z.width, :] = pack.astype(BF16)
    pack_ref[z.width :, :] = second_ref[...].astype(BF16)


def sum_pairs(parts):
    parts = [part.astype(F32) for part in parts]
    while len(parts) > 1:
        parts = [parts[i] + parts[i + 1] for i in range(0, len(parts), 2)]
    return parts[0]


def sum_over(value, axis):
    size = lax.axis_size(axis)
    if size > 4:
        return lax.psum(value.astype(F32), axis)
    return sum_pairs([value] + [swap(value, axis, step) for step in range(1, size)])


def core_sum_kernel(keep_ref, got_ref, mine_ref, send_ref):
    x = lax.axis_index("seq") >> 1
    mine_ref[...] = keep_ref[x].astype(F32) + got_ref[x].astype(F32)
    send_ref[...] = (keep_ref[1 - x].astype(F32) + got_ref[1 - x].astype(F32)).astype(BF16)


def x_sum_kernel(keep_ref, got_ref, mine_ref, send_ref):
    chan = lax.axis_index("chan")
    rows = mine_ref.shape[0]
    for base, out in ((chan, mine_ref), (1 - chan, send_ref)):
        at = pl.ds(pl.multiple_of(base * rows, rows), rows)
        out[...] = (keep_ref[at, :] + got_ref[at, :].astype(F32)).astype(out.dtype)


def y_sum_kernel(keep_ref, got_ref, *outs):
    rows = outs[0].shape[0]
    dp = lax.axis_index("dp")
    for step, out in enumerate(outs):
        at = pl.ds(pl.multiple_of((dp ^ step) * rows, rows), rows)
        out[...] = (keep_ref[at, :] + got_ref[at, :].astype(F32)).astype(BF16)


def z_sum_kernel(own_ref, a_ref, b_ref, c_ref, out_ref):
    parts = [ref[...].astype(F32) for ref in (own_ref, a_ref, b_ref, c_ref)]
    out_ref[...] = ((parts[0] + parts[1]) + (parts[2] + parts[3])).astype(BF16)


def z_join_kernel(own_ref, a_ref, b_ref, c_ref, out_ref):
    rows = own_ref.shape[0]
    dp = lax.axis_index("dp")
    for step, ref in enumerate((own_ref, a_ref, b_ref, c_ref)):
        out_ref[pl.ds(pl.multiple_of((dp ^ step) * rows, rows), rows), :] = ref[...]


def y_join_kernel(own_ref, got_ref, out_ref):
    rows = own_ref.shape[0]
    chan = lax.axis_index("chan")
    for base, ref in ((chan, own_ref), (1 - chan, got_ref)):
        out_ref[pl.ds(pl.multiple_of(base * rows, rows), rows), :] = ref[...].astype(F32)


def sum_first(keep, send):
    _, rows, width = keep.shape
    got = swap(send, "seq", 1)
    mine, send = call(
        core_sum_kernel, [struct((rows, width), F32), struct((rows, width))], [keep, got], name="core_sum"
    )
    got = swap(send, "seq", 2)
    rows //= 2
    mine, send = call(
        x_sum_kernel, [struct((rows, width), F32), struct((rows, width))], [mine, got], name="x_sum"
    )
    got = swap(send, "chan", 1)
    rows //= 4
    parts = call(y_sum_kernel, [struct((rows, width))] * 4, [mine, got], name="y_sum")
    parts = [parts[0]] + [swap(parts[step], "dp", step) for step in range(1, 4)]
    (own,) = call(z_sum_kernel, [struct((rows, width))], parts, name="z_sum")
    parts = [own] + [swap(own, "dp", step) for step in range(1, 4)]
    rows *= 4
    (own,) = call(z_join_kernel, [struct((rows, width))], parts, name="z_join")
    got = swap(own, "chan", 1)
    (full,) = call(y_join_kernel, [struct((2 * rows, width), F32)], [own, got], name="y_join")
    return full


def per_device(tokens, chan_in, chan_out, seq_in, seq_out, head_grad, masked):
    seq_count = lax.axis_size("seq")
    chan_index = lax.axis_index("chan")
    tokens, head_grad = tokens[0], head_grad[0]
    z = Sizes(tokens, chan_in, seq_count)
    wide = (z.positions, z.width)
    packed = (z.half, 2 * z.part)
    bind = functools.partial
    macs = 2 * z.positions * z.width

    own, other = call(
        bind(first_mix_kernel, z), [struct(packed)] * 2, [tokens, chan_in], flops=macs * 768, name="first_mix"
    )
    got = swap(other, "chan", 1)

    factors = lax.dynamic_slice_in_dim(chan_out, chan_index * z.my_lanes, z.my_lanes, 0)
    factors = jnp.transpose(factors, (1, 0, 2)).reshape(z.blocks * z.my_lanes, z.blocks)
    upstream, turned, dense = call(
        bind(prepare_kernel, z),
        [struct(wide), struct(seq_in.shape), struct((z.blocks * z.my_lanes, z.width))],
        [head_grad, masked, seq_in, factors],
        flops=macs * 64,
        name="prepare",
    )
    rows_scratch = pltpu.VMEM((z.seq, z.group, z.width), BF16)
    pad_scratch = pltpu.VMEM((3 * z.part, z.width), BF16)
    outs = call(
        bind(channel_mix_kernel, z),
        [struct(wide)] * 2 + block_outs(z),
        [own, got, dense, upstream, seq_out],
        [pad_scratch, rows_scratch],
        flops=macs * 1024,
        name="channel_mix",
    )
    mix, gated, row_grad = outs[0], outs[1], outs[2:]
    row_grad = exchange_blocks(z, row_grad)
    row_mix = call(
        bind(row_mix_kernel, z), block_outs(z), [turned, mix], [rows_scratch], flops=macs * 1024, name="row_mix"
    )
    spread = exchange_blocks(z, row_mix)
    (gate,) = call(bind(gate_kernel, z), [struct(wide, F32)], [mix, upstream], flops=macs * 64, name="gate")
    count = len(row_grad)
    if z.direct:
        outs = [struct((2, z.group, seq_in.shape[1]))] * 2
    else:
        outs = [struct(seq_in.shape, F32)]
    seq_part, *first_parts = call(
        bind(seq_grad_kernel, z, count),
        [struct(wide, F32)] + outs,
        [seq_in, mix] + list(row_grad),
        [rows_scratch],
        flops=macs * 2048,
        name="seq_grad",
    )
    mix_grad, own_grad, other_grad = call(
        bind(mix_grad_kernel, z, count),
        [struct(wide)] + [struct(packed)] * 2,
        [gate, seq_part, dense, seq_out] + list(spread),
        [rows_scratch, pad_scratch],
        flops=macs * 1024,
        name="mix_grad",
    )
    got_grad = swap(other_grad, "chan", 1)
    out_part, second_part = call(
        bind(out_grad_kernel, z, count),
        [struct((z.width, PACK_LANES), F32), struct((max(16, z.seq), PACK_LANES), F32)],
        [own, got, mix_grad, gated] + list(spread),
        [rows_scratch, pltpu.VMEM((2 * z.part, z.width), F32)],
        flops=macs * 1024,
        name="out_grad",
    )
    x_grad, pack = call(
        bind(in_grad_kernel, z),
        [struct(wide), struct((z.width + second_part.shape[0], PACK_LANES))],
        [tokens, chan_in, own_grad, got_grad, out_part, second_part],
        flops=macs * 1536,
        name="in_grad",
    )
    if z.direct:
        first_rows = sum_first(*first_parts)
    else:
        first_rows = lax.psum_scatter(first_parts[0], "seq", scatter_dimension=0, tiled=True)
        first_rows = lax.psum(first_rows, ("dp", "chan"))
    pack = sum_over(pack, "seq").astype(BF16)
    pack = sum_over(pack, "dp").astype(BF16)
    there = swap(pack, "chan", 1)
    both = jnp.stack([jnp.where(chan_index == 0, pack, there), jnp.where(chan_index == 0, there, pack)])
    both = both.astype(F32)
    in_sum = both[:, : z.width, : z.block].reshape(z.blocks, z.block, z.block)
    out_sum = both[:, : z.width, z.block : z.block + z.blocks]
    out_sum = out_sum.reshape(2, z.blocks, z.my_lanes, z.blocks)
    out_sum = jnp.transpose(out_sum, (0, 2, 1, 3)).reshape(z.block, z.blocks, z.blocks)
    second_sum = both[0, z.width : z.width + z.seq, : z.seq] + both[1, z.width : z.width + z.seq, : z.seq]
    return (x_grad[None], in_sum, out_sum, first_rows, second_sum)


def solution(mesh):
    in_specs = (P("dp", "seq", "chan"), P(), P(), P(), P(), P("dp", "seq", "chan"), P("dp", "seq"))
    out_specs = (P("dp", "seq", "chan"), P(), P(), P("seq", None), P())
    return jax.shard_map(
        per_device, mesh=mesh, in_specs=in_specs, out_specs=out_specs, check_vma=False
    )
```

```python
import functools

import jax
import jax.numpy as jnp
from jax import lax
from jax.experimental import pallas as pl
from jax.experimental.pallas import tpu as pltpu
from jax.sharding import PartitionSpec as P

F32 = jnp.float32
BF16 = jnp.bfloat16
VMEM_LIMIT = 24 * 1024 * 1024
PACK_LANES = 128
MIX_FLOPS = 600000000
OUT_FLOPS = 1
PACK_SUM_FLOPS = 1
X_FLOPS = 1
OWN_X_FLOPS = 4000000000


def dot(lhs, rhs, lhs_dim=1, rhs_dim=0):
    return lax.dot_general(
        lhs, rhs, (((lhs_dim,), (rhs_dim,)), ((), ())), preferred_element_type=F32
    )


def dot_exact(lhs, rhs, lhs_dim=1, rhs_dim=0):
    return lax.dot_general(
        lhs,
        rhs,
        (((lhs_dim,), (rhs_dim,)), ((), ())),
        precision=lax.Precision.HIGHEST,
        preferred_element_type=F32,
    )


def rows_of(shape):
    return lax.broadcasted_iota(jnp.int32, shape, 0)


def columns_of(shape):
    return lax.broadcasted_iota(jnp.int32, shape, 1)


def call(body, outs, args, scratch=(), flops=1, name=None):
    nbytes = sum(a.size * a.dtype.itemsize for a in list(args) + list(outs))
    return pl.pallas_call(
        body,
        out_shape=tuple(outs),
        in_specs=[pl.BlockSpec(memory_space=pltpu.VMEM)] * len(args),
        out_specs=tuple([pl.BlockSpec(memory_space=pltpu.VMEM)] * len(outs)),
        scratch_shapes=list(scratch),
        compiler_params=pltpu.CompilerParams(vmem_limit_bytes=VMEM_LIMIT),
        cost_estimate=pl.CostEstimate(flops=flops, bytes_accessed=1, transcendentals=0),
        name=name,
    )(*args)


def struct(shape, dtype=BF16):
    return jax.ShapeDtypeStruct(shape, dtype)


class Sizes:
    def __init__(self, tokens, chan_in, seq_count):
        self.positions, self.width = tokens.shape
        self.blocks, self.block = chan_in.shape[0], chan_in.shape[1]
        self.my_blocks = self.blocks // 2
        self.my_lanes = self.block // 2
        self.half = self.positions // 2
        self.quarter = self.positions // 4
        self.part = self.my_blocks * self.my_lanes
        self.seq = seq_count
        self.group = self.positions // seq_count
        self.direct = seq_count == 4
        self.fronts = 4 if self.direct else 2
        self.front = self.positions // self.fronts
        self.piece = self.group // self.fronts
        self.step = min(64, self.piece)
        self.chunk = self.step * seq_count
        self.pack_in = self.width // 2
        self.pack_out = 16 * (self.width // PACK_LANES)
        self.pack_rows = self.pack_in + self.pack_out + max(16, seq_count)
        self.share = self.pack_rows // seq_count


def lane_masks(z):
    shape = (z.width, 2 * z.part)
    row, column = rows_of(shape), columns_of(shape)
    left = column < z.part
    place = jnp.where(left, column, column - z.part)
    same = (row // z.block) == (place // z.my_lanes)
    return same & left, same & jnp.logical_not(left)


def in_matrices(z, in_ref, lane_base):
    chan = lax.axis_index("chan")
    blocks = in_ref[pl.ds(chan * z.my_blocks, z.my_blocks)].reshape(z.width, z.block)
    column = columns_of((z.block, 2 * z.part))
    pick = rows_of((z.block, 2 * z.part)) == lane_base + (column & (z.my_lanes - 1))
    spread = dot(blocks, pick.astype(BF16))
    left, right = lane_masks(z)
    return jnp.where(left, spread, 0.0).astype(BF16), jnp.where(right, spread, 0.0).astype(BF16)


def lane_of_channel(z, shape, axis):
    index = lax.broadcasted_iota(jnp.int32, shape, axis)
    lane = (index * 5462) >> 16
    return lane, index - z.blocks * lane


def out_mask(z):
    shape = (z.blocks * z.my_lanes, z.width)
    lane, _ = lane_of_channel(z, shape, 1)
    return (rows_of(shape) & (z.my_lanes - 1)) == lane


def out_matrix(z, factors):
    shape = (z.blocks, z.width)
    _, entry = lane_of_channel(z, shape, 1)
    spread = dot(factors, (rows_of(shape) == entry).astype(BF16))
    return jnp.where(out_mask(z), spread, 0.0).astype(BF16)


def position_masks(z):
    shape = (z.chunk, z.chunk)
    row, column = rows_of(shape), columns_of(shape)
    same = (row & (z.step - 1)) == (column // z.seq)
    blocks = (z.chunk, z.seq)
    of_a = (rows_of(blocks) // z.step) == columns_of(blocks)
    turned = (z.seq, z.chunk)
    of_a2 = (columns_of(turned) & (z.seq - 1)) == rows_of(turned)
    return same, of_a, of_a2


def position_matrix(z, factor):
    same, of_a, of_a2 = position_masks(z)
    by_row = dot(of_a.astype(BF16), factor).astype(BF16)
    return jnp.where(same, dot(by_row, of_a2.astype(BF16)), 0.0).astype(BF16)


def split_blocks(z, full_ref, refs):
    if not z.direct:
        refs[0][...] = full_ref[...]
        return
    mine = lax.axis_index("seq")
    stay_ref, mate_ref, far_ref = refs
    stay_ref[...] = full_ref[mine]
    mate_ref[...] = full_ref[mine ^ 1]
    far_ref[0] = full_ref[mine ^ 2]
    far_ref[1] = full_ref[mine ^ 3]


def block_outs(z, rows):
    if not z.direct:
        return [struct((z.seq, rows, z.width))]
    return [struct((rows, z.width))] * 2 + [struct((2, rows, z.width))]


def own_mate_kernel(*refs):
    rows, out_ref = refs[0].shape[0], refs[-1]
    for c, ref in enumerate(refs[:-1]):
        out_ref[c * rows : (c + 1) * rows, :] = ref[...]


def mate_kernel(count, *refs):
    rows, out_ref = refs[0].shape[1], refs[-1]
    for c in range(count):
        out_ref[c * rows : (c + 1) * rows, :] = refs[c][1]


def exchange_blocks(z, chunks, fars, after):
    if not z.direct:
        return [lax.all_to_all(c[0], "seq", split_axis=0, concat_axis=0, tiled=True) for c in chunks]
    whole = [struct((z.group, z.width))]
    mates = [mate for _, mate, _ in chunks]
    if len(mates) > 1:
        mates = call(own_mate_kernel, whole, mates, name="own_mate")
    for_mate = call(functools.partial(mate_kernel, len(chunks)), whole, fars + [after], name="mate")
    return [stay for stay, _, _ in chunks] + fars + [swap(mates[0], "seq", 1), swap(for_mate[0], "seq", 1)]


def send_far(z, blocks):
    return swap(blocks[2], "seq", 2) if z.direct else blocks[0]


def join_blocks(z, refs, full_ref):
    count = len(refs) // 2 - 1 if z.direct else len(refs)
    size = z.group // count
    mine = lax.axis_index("seq")
    for c in range(count):
        rows = slice(c * size, (c + 1) * size)
        if not z.direct:
            full_ref[:, rows, :] = refs[c][...]
            continue
        full_ref[mine, rows, :] = refs[c][...]
        full_ref[mine ^ 1, rows, :] = refs[2 * count][rows, :]
        full_ref[mine ^ 2, rows, :] = refs[count + c][0]
        full_ref[mine ^ 3, rows, :] = refs[2 * count + 1][rows, :]


def swap(value, axis, step):
    size = lax.axis_size(axis)
    return lax.ppermute(value, axis, [(i, i ^ step) for i in range(size)])


def swap_both(value, chan_step, seq_step):
    seq = lax.axis_size("seq")
    pairs = [
        (c * seq + s, (c ^ chan_step) * seq + (s ^ seq_step))
        for c in range(lax.axis_size("chan"))
        for s in range(seq)
    ]
    return lax.ppermute(value, ("chan", "seq"), pairs)


def quarters(z, ref, c):
    low = ref[c * z.half : c * z.half + z.quarter, :]
    return low, ref[c * z.half + z.quarter : (c + 1) * z.half, :]


def front_rows(z, ref, c):
    middle = c * z.front + z.front // 2
    return ref[c * z.front : middle, :], ref[middle : (c + 1) * z.front, :]


def first_kernel(z, c, x_ref, in_ref, out_ref):
    chan = lax.axis_index("chan")
    lower, upper = in_matrices(z, in_ref, (1 - chan) * z.my_lanes)
    low, high = front_rows(z, x_ref, c)
    out_ref[...] = (dot(low, lower) + dot(high, upper)).astype(BF16)


def prepare_kernel(z, x_ref, in_ref, head_ref, mask_ref, seq_ref, out_ref, after_ref, *outs):
    own_refs, (up_ref, turn_ref, pad_ref, win_ref) = outs[: z.fronts], outs[z.fronts :]
    chan = lax.axis_index("chan")
    lower, upper = in_matrices(z, in_ref, chan * z.my_lanes)
    win_ref[0], win_ref[1] = lower, upper
    win_ref[2], win_ref[3] = in_matrices(z, in_ref, (1 - chan) * z.my_lanes)
    for c, ref in enumerate(own_refs):
        low, high = front_rows(z, x_ref, c)
        ref[...] = (dot(low, lower) + dot(high, upper)).astype(BF16)
    lines = jnp.broadcast_to(mask_ref[...].astype(F32), (16, z.positions)).astype(BF16)
    ones = jnp.full((16, z.width), 1.0 / 16.0, BF16)
    mask = dot(lines, ones, 0, 0)
    up_ref[...] = (mask * head_ref[...].astype(F32)).astype(BF16)
    turn_ref[...] = jnp.transpose(seq_ref[...])
    pad_ref[...] = jnp.zeros_like(pad_ref)
    dense = out_matrix(z, out_ref[...])
    for base in range(2):
        pad_ref[base ^ chan, z.part : 2 * z.part, :] = dense[base * z.part : (base + 1) * z.part, :]


def channel_mix_kernel(z, c, own_ref, got_ref, pad_ref, up_ref, so_ref, *rest):
    mix_ref, gated_ref = rest[:2]
    refs, rows_ref = rest[2:-1], rest[-1]
    own, got = own_ref[...], got_ref[...]
    rows = z.front // 2
    low = dot(own, pad_ref[0, z.part :, :]) + dot(got, pad_ref[1, z.part :, :])
    high = dot(own, pad_ref[0, : 2 * z.part, :]) + dot(got, pad_ref[1, : 2 * z.part, :])
    for at, values in ((0, low), (rows, high)):
        rounded = values.astype(BF16)
        mix_ref[at : at + rows, :] = rounded
        mixed = rounded.astype(F32)
        upstream = up_ref[c * z.front + at : c * z.front + at + rows, :].astype(F32)
        gated = upstream * (mixed * jax.nn.sigmoid(mixed))
        gated_ref[at : at + rows, :] = gated.astype(BF16)
    matrix = position_matrix(z, so_ref[...])
    for j in range(z.front // z.chunk):
        out = dot(matrix, gated_ref[j * z.chunk : (j + 1) * z.chunk, :]).astype(BF16)
        rows_ref[:, j * z.step : (j + 1) * z.step, :] = out.reshape(z.seq, z.step, z.width)
    split_blocks(z, rows_ref, refs)


def row_mix_kernel(z, turn_ref, *rest):
    mixes, (all0_ref, all1_ref), refs, rows_ref = rest[: z.fronts], rest[z.fronts :][:2], rest[z.fronts + 2 : -1], rest[-1]
    per_half = z.fronts // 2
    for c, mix_ref in enumerate(mixes):
        at = (c % per_half) * z.front
        (all0_ref, all1_ref)[c // per_half][at : at + z.front, :] = mix_ref[...]
    out = dot(turn_ref[:, : z.half], all0_ref[...]) + dot(turn_ref[:, z.half :], all1_ref[...])
    rows_ref[...] = out.astype(BF16).reshape(z.seq, z.group, z.width)
    split_blocks(z, rows_ref, refs)


def seq_grad_kernel(z, count, mix0_ref, mix1_ref, *rest):
    refs, all_ref, outs, rows_ref = rest[:count], rest[count], rest[count + 1 : -1], rest[-1]
    join_blocks(z, refs, rows_ref)
    all_ref[...] = rows_ref[...].reshape(z.positions, z.width)
    if not z.direct:
        for c, mix_ref in enumerate((mix0_ref, mix1_ref)):
            outs[0][c * z.half : (c + 1) * z.half, :] = dot(mix_ref[...], all_ref[...], 1, 1)
        return
    core_products(z, 1 - (lax.axis_index("seq") & 1), (mix0_ref, mix1_ref), all_ref, outs)


def core_products(z, core, mixes, all_ref, outs):
    lines = z.group // 2
    for k, out in enumerate(outs):
        at = pl.multiple_of(core * z.group + (k & 1) * lines, lines)
        out[...] = dot(mixes[k >> 1][pl.ds(at, lines), :], all_ref[...], 1, 1).astype(BF16)


def own_product_kernel(z, mix0_ref, mix1_ref, all_ref, *outs):
    core_products(z, lax.axis_index("seq") & 1, (mix0_ref, mix1_ref), all_ref, outs)


def seq_part_kernel(z, seq_ref, rows_ref, mix0_ref, mix1_ref, up_ref, after_ref, part_ref, gate_ref):
    part_ref[...] = dot(seq_ref[...], rows_ref[...])
    for c, mix_ref in enumerate((mix0_ref, mix1_ref)):
        at = slice(c * z.half, (c + 1) * z.half)
        mixed = mix_ref[...].astype(F32)
        sig = jax.nn.sigmoid(mixed)
        gate_ref[at, :] = up_ref[at, :].astype(F32) * (sig * (1.0 + mixed * (1.0 - sig)))


def turn_kernel(z, x_ref, *rest):
    owns, gots = rest[: z.fronts], rest[z.fronts : 2 * z.fronts]
    xt_ref, ot_ref, gt_ref = rest[2 * z.fronts + 1 :]
    xt_ref[...] = jnp.transpose(x_ref[...])
    rows = z.front // 2
    for refs, out_ref in ((owns, ot_ref), (gots, gt_ref)):
        for c, ref in enumerate(refs):
            out_ref[:, c * rows : (c + 1) * rows] = jnp.transpose(ref[...])


def mix_grad_kernel(z, gate_ref, part_ref, pad_ref, so_ref, *rest):
    refs, (mixg_ref, own_ref, other_ref, spread_ref, joined_ref) = rest[:-5], rest[-5:]
    matrix = position_matrix(z, so_ref[...])
    join_blocks(z, refs, joined_ref)
    for j in range(z.positions // z.chunk):
        rows = joined_ref[:, j * z.step : (j + 1) * z.step, :].reshape(z.chunk, z.width)
        at = slice(j * z.chunk, (j + 1) * z.chunk)
        spread_ref[at, :] = rows
        gate = gate_ref[at, :] * dot(matrix, rows, 0, 0)
        mixg_ref[at, :] = (gate + part_ref[at, :]).astype(BF16)
    for c in range(2):
        low, high = quarters(z, mixg_ref, c)
        for base, ref in ((1, other_ref), (0, own_ref)):
            first = dot(low, pad_ref[base, z.part :, :], 1, 1)
            total = first + dot(high, pad_ref[base, : 2 * z.part, :], 1, 1)
            ref[c * z.quarter : (c + 1) * z.quarter, :] = total.astype(BF16)


def in_products(z, xt_ref, grad_ref, lane_base):
    low = high = None
    for c in range(2):
        at = c * z.half
        grad = grad_ref[c * z.quarter : (c + 1) * z.quarter, :]
        first = dot(xt_ref[:, at : at + z.quarter], grad)
        second = dot(xt_ref[:, at + z.quarter : at + z.half], grad)
        low = first if low is None else low + first
        high = second if high is None else high + second
    left, right = lane_masks(z)
    products = jnp.where(left, low, jnp.where(right, high, 0.0)).astype(BF16)
    shape = (2 * z.part, PACK_LANES)
    lane = lane_base + (rows_of(shape) & (z.my_lanes - 1))
    column = columns_of(shape)
    packed = dot(products[: z.pack_in, :], (column == lane).astype(BF16))
    return packed + dot(products[z.pack_in :, :], (column == lane + z.block).astype(BF16))


def out_grad_kernel(z, *rest):
    ot_ref, gt_ref, xt_ref, mixg_ref, owng_ref = rest[:5]
    gateds, spread_ref = rest[5 : 5 + z.fronts], rest[5 + z.fronts]
    in_ref, small_ref = rest[6 + z.fronts :]
    chan = lax.axis_index("chan")
    in_ref[...] = in_products(z, xt_ref, owng_ref, chan * z.my_lanes)
    shape = (16, z.width)
    _, entry = lane_of_channel(z, shape, 1)
    to_entry = (rows_of(shape) == entry).astype(BF16)
    shape = (z.part, z.width)
    lane, _ = lane_of_channel(z, shape, 1)
    mask = (rows_of(shape) & (z.my_lanes - 1)) == lane
    sides = []
    for turned_ref in (ot_ref, gt_ref):
        kept = None
        for c in range(z.fronts):
            low, high = front_rows(z, mixg_ref, c)
            at = slice(c * z.front // 2, (c + 1) * z.front // 2)
            both = dot(turned_ref[: z.part, at], low) + dot(turned_ref[z.part :, at], high)
            kept = both if kept is None else kept + both
        sides.append(dot(to_entry, jnp.where(mask, kept, 0.0).astype(BF16), 1, 1))
    both = jnp.concatenate(
        [jnp.where(chan == 0, sides[0], sides[1]), jnp.where(chan == 0, sides[1], sides[0])], axis=1
    ).astype(BF16)
    for j in range(z.width // PACK_LANES):
        small_ref[j * 16 : (j + 1) * 16, :] = both[:, j * PACK_LANES : (j + 1) * PACK_LANES]
    same, of_a, of_a2 = position_masks(z)
    total = jnp.zeros((z.chunk, z.chunk), F32)
    for c, gated_ref in enumerate(gateds):
        for j in range(z.front // z.chunk):
            at = c * z.front + j * z.chunk
            gated = gated_ref[j * z.chunk : (j + 1) * z.chunk, :]
            total = total + dot(spread_ref[at : at + z.chunk, :], gated, 1, 1)
    total = jnp.where(same, total, 0.0)
    shape = (z.chunk, PACK_LANES)
    to_a2 = ((rows_of(shape) & (z.seq - 1)) == columns_of(shape)).astype(F32)
    tall = (max(16, z.seq), z.chunk)
    to_a = ((columns_of(tall) // z.step) == rows_of(tall)).astype(F32)
    small_ref[z.pack_out :, :] = dot_exact(to_a, dot_exact(total, to_a2)).astype(BF16)


def pack_kernel(z, xt_ref, got_ref, in_ref, small_ref, after0_ref, after1_ref, *rest):
    outs, pack_ref = rest[:-1], rest[-1]
    there = (1 - lax.axis_index("chan")) * z.my_lanes
    pack_ref[: z.pack_in, :] = (in_ref[...] + in_products(z, xt_ref, got_ref, there)).astype(BF16)
    pack_ref[z.pack_in :, :] = small_ref[...]
    if not z.direct:
        outs[0][...] = pack_ref[...]
        return
    mine = lax.axis_index("seq")
    for step, ref in enumerate(outs):
        ref[...] = pack_ref[pl.ds(pl.multiple_of((mine ^ step) * z.share, z.share), z.share), :]


def own_x_grad_kernel(z, win_ref, own_ref, after_ref, part_ref, token_ref):
    for c in range(2):
        rows = slice(c * z.quarter, (c + 1) * z.quarter)
        for side in range(2):
            at = c * z.half + side * z.quarter
            part_ref[at : at + z.quarter, :] = dot(own_ref[rows, :], win_ref[side], 1, 1)
    token_ref[...] = part_ref[: token_ref.shape[0], : token_ref.shape[1]]


def x_grad_kernel(z, win_ref, part_ref, got_ref, after_ref, xg_ref, token_ref):
    for c in range(2):
        rows = slice(c * z.quarter, (c + 1) * z.quarter)
        for side in range(2):
            at = slice(c * z.half + side * z.quarter, c * z.half + (side + 1) * z.quarter)
            total = part_ref[at, :] + dot(got_ref[rows, :], win_ref[2 + side], 1, 1)
            xg_ref[at, :] = total.astype(BF16)
    token_ref[...] = xg_ref[: token_ref.shape[0], : token_ref.shape[1]]


def unpack(z, sides, in_ref, out_ref, second_ref):
    per_side = z.my_blocks // 2
    for half, side in enumerate(sides):
        lanes = slice(half * z.my_lanes, (half + 1) * z.my_lanes)
        for b in range(z.my_blocks):
            at, base = (b % per_side) * z.block, (b // per_side) * z.block
            in_ref[half * z.my_blocks + b] = side[at : at + z.block, base : base + z.block]
        for b in range(z.blocks):
            at = z.pack_in + 16 * (b * z.my_lanes // PACK_LANES)
            base = b * z.my_lanes % PACK_LANES
            out_ref[b, :, lanes] = side[at : at + z.blocks, base : base + z.my_lanes]
    at = z.pack_in + z.pack_out
    second_ref[...] = sides[0][at : at + z.seq, : z.seq] + sides[1][at : at + z.seq, : z.seq]


def sum_pairs(parts):
    parts = [part.astype(F32) for part in parts]
    while len(parts) > 1:
        parts = [parts[i] + parts[i + 1] for i in range(0, len(parts), 2)]
    return parts[0]


def pair_sum_kernel(a_ref, b_ref, c_ref, d_ref, out_ref):
    out_ref[...] = sum_pairs([a_ref[...], b_ref[...], c_ref[...], d_ref[...]]).astype(out_ref.dtype)


def core_sum_kernel(*refs):
    keeps, gots, (keep0_ref, keep1_ref, send0_ref, send1_ref, all_ref) = refs[:4], refs[4:8], refs[8:]
    x, chan = lax.axis_index("seq") >> 1, lax.axis_index("chan")
    rows, half = all_ref.shape[1], all_ref.shape[2] // 2
    for k in range(4):
        all_ref[k] = keeps[k][...].astype(F32) + gots[k][...].astype(F32)
    for step in range(2):
        at = slice(step * rows, (step + 1) * rows)
        keep0_ref[at, :] = all_ref[2 * (x ^ step) + chan, :, :half]
        send0_ref[at, :] = all_ref[2 * (x ^ step) + (1 - chan), :, :half].astype(BF16)
        keep1_ref[at, :] = all_ref[2 * x + (chan ^ step), :, half:]
        send1_ref[at, :] = all_ref[2 * (1 - x) + (chan ^ step), :, half:].astype(BF16)


def side_sum_kernel(keep0_ref, got0_ref, keep1_ref, got1_ref, after_ref, mine_ref, send0_ref, send1_ref):
    rows, half = send0_ref.shape
    mine_ref[:, :half] = keep0_ref[:rows, :] + got0_ref[:rows, :].astype(F32)
    mine_ref[:, half:] = keep1_ref[:rows, :] + got1_ref[:rows, :].astype(F32)
    send0_ref[...] = (keep0_ref[rows:, :] + got0_ref[rows:, :].astype(F32)).astype(BF16)
    send1_ref[...] = (keep1_ref[rows:, :] + got1_ref[rows:, :].astype(F32)).astype(BF16)


def plane_sum_kernel(rows, keep_ref, got0_ref, got1_ref, after_ref, *outs):
    dp = lax.axis_index("dp")
    blocks = keep_ref.shape[1] // PACK_LANES
    for step, out in enumerate(outs):
        at = pl.ds(pl.multiple_of((dp ^ step) * rows, rows), rows)
        for j in range(blocks):
            got_ref, there = (got0_ref, j) if j < blocks // 2 else (got1_ref, j - blocks // 2)
            got = got_ref[at, there * PACK_LANES : (there + 1) * PACK_LANES].astype(F32)
            total = keep_ref[at, j * PACK_LANES : (j + 1) * PACK_LANES] + got
            out[j * rows : (j + 1) * rows, :] = total.astype(BF16)


def pack_sum_kernel(a_ref, b_ref, c_ref, d_ref, out_ref):
    out_ref[...] = sum_pairs([a_ref[...], b_ref[...], c_ref[...], d_ref[...]]).astype(BF16)


def z_sum_kernel(own_ref, a_ref, b_ref, c_ref, small_ref, out_ref):
    rows = own_ref.shape[0]
    out_ref[:rows, :] = sum_pairs([own_ref[...], a_ref[...], b_ref[...], c_ref[...]]).astype(BF16)
    out_ref[rows:, :] = small_ref[...]


def pass_on_kernel(line_ref, after_ref, out_ref):
    out_ref[...] = line_ref[...]


def line_sum_kernel(z, *refs):
    out_ref = refs[8]
    rows = refs[0].shape[0] - z.share
    for there in range(2):
        at = pl.multiple_of((lax.axis_index("chan") ^ there) * z.share, z.share)
        total = sum_pairs([ref[rows:, :] for ref in refs[4 * there : 4 * there + 4]])
        out_ref[pl.ds(at, z.share), :] = total.astype(BF16)


def last_kernel(z, rows, *refs):
    lines, smalls = (refs[:4], refs[4:8]), refs[8:12]
    first_ref, in_ref, out_ref, second_ref, all_ref = refs[12:]
    chan, dp, mine = lax.axis_index("chan"), lax.axis_index("dp"), lax.axis_index("seq")
    for there in range(2):
        for step in range(4):
            to = pl.ds(pl.multiple_of(((chan ^ there) * 4 + (dp ^ step)) * rows, rows), rows)
            for j in range(first_ref.shape[1] // PACK_LANES):
                lanes = slice(j * PACK_LANES, (j + 1) * PACK_LANES)
                values = lines[there][step][j * rows : (j + 1) * rows, :]
                first_ref[to, lanes] = values.astype(F32)
    for step in range(4):
        at = pl.ds(pl.multiple_of((mine ^ step) * z.share, z.share), z.share)
        for half in range(2):
            values = smalls[step][half * z.share : (half + 1) * z.share, :]
            all_ref[half, at, :] = values.astype(F32)
    unpack(z, [all_ref[0], all_ref[1]], in_ref, out_ref, second_ref)


def pack_last_kernel(z, own_ref, got_ref, in_ref, out_ref, second_ref):
    chan = lax.axis_index("chan")
    own, got = own_ref[...], got_ref[...]
    unpack(z, [jnp.where(chan == 0, own, got), jnp.where(chan == 0, got, own)], in_ref, out_ref, second_ref)


def sum_cores(keeps, sends):
    rows, width = sends[0].shape
    half = (2 * rows, width // 2)
    return call(
        core_sum_kernel,
        [struct(half, F32)] * 2 + [struct(half)] * 2,
        list(keeps) + [swap(block, "seq", 1) for block in sends],
        [pltpu.VMEM((4, rows, width), F32)],
        name="core_sum",
    )


def sum_factors(z, core_sums, pack_after, mix_after, small_after, outs):
    keep0, keep1, send0, send1 = core_sums
    rows, width = keep0.shape[0] // 2, 2 * keep0.shape[1]
    bind = functools.partial
    mine, send0, send1 = call(
        side_sum_kernel,
        [struct((rows, width), F32)] + [struct((rows, width // 2))] * 2,
        [keep0, swap(send0, "chan", 1), keep1, swap(send1, "seq", 2), mix_after],
        name="side_sum",
    )
    lines = rows // 4
    tall = lines * (width // PACK_LANES)
    parts = call(
        bind(plane_sum_kernel, lines),
        [struct((tall, PACK_LANES))] * 4,
        [mine, swap(send0, "seq", 2), swap(send1, "chan", 1), small_after],
        name="plane_sum",
    )
    packs, x_grad, x_done = pack_after(parts[0])
    packs = [packs[0]] + [swap(packs[step], "seq", step) for step in range(1, 4)]
    (pack,) = call(
        pack_sum_kernel, [struct((z.share, PACK_LANES))], packs, flops=PACK_SUM_FLOPS, name="pack_sum"
    )
    parts = [parts[0]] + [swap(parts[step], "dp", step) for step in range(1, 4)]
    (own,) = call(
        z_sum_kernel,
        [struct((tall + z.share, PACK_LANES))],
        list(parts) + [pack],
        name="z_sum",
    )
    own_lines = [own] + [swap(own, "dp", step) for step in range(1, 4)]
    passed = list(own_lines)
    (passed[3],) = call(pass_on_kernel, [struct(own.shape)], [own_lines[3], x_done], name="pass_on")
    got_lines = [swap(line, "chan", 1) for line in passed]
    (small,) = call(
        bind(line_sum_kernel, z), [struct((2 * z.share, PACK_LANES))], own_lines + got_lines, name="line_sum"
    )
    smalls = [small] + [swap(small, "seq", step) for step in range(1, 4)]
    return x_grad, *call(
        bind(last_kernel, z, lines),
        [struct((8 * lines, width), F32)] + outs,
        own_lines + got_lines + smalls,
        [pltpu.VMEM((2, z.pack_rows, PACK_LANES), F32)],
        name="last",
    )


def sum_factors_plain(z, first, pack, outs):
    first = lax.psum_scatter(first, "seq", scatter_dimension=0, tiled=True)
    first = lax.psum(first, ("dp", "chan"))
    pack = lax.psum(pack.astype(F32), ("dp", "seq"))
    got = swap(pack, "chan", 1)
    return [first] + list(call(functools.partial(pack_last_kernel, z), outs, [pack, got], name="last"))


def per_device(tokens, chan_in, chan_out, seq_in, seq_out, head_grad, masked):
    seq_count = lax.axis_size("seq")
    chan_index = lax.axis_index("chan")
    tokens, head_grad = tokens[0], head_grad[0]
    z = Sizes(tokens, chan_in, seq_count)
    wide, chunk = (z.positions, z.width), (z.half, z.width)
    front = (z.front // 2, 2 * z.part)
    bind = functools.partial

    others = [
        call(bind(first_kernel, z, c), [struct(front)], [tokens, chan_in], name="first_mix")[0]
        for c in range(z.fronts)
    ]
    gots = [swap(other, "chan", 1) for other in others]

    factors = lax.dynamic_slice_in_dim(chan_out, chan_index * z.my_lanes, z.my_lanes, 0)
    factors = jnp.transpose(factors, (1, 0, 2)).reshape(z.blocks * z.my_lanes, z.blocks)
    *owns, upstream, turned, pads, in_mats = call(
        bind(prepare_kernel, z),
        [struct(front)] * z.fronts
        + [
            struct(wide),
            struct(seq_in.shape),
            struct((2, 3 * z.part, z.width)),
            struct((4, z.width, 2 * z.part)),
        ],
        [tokens, chan_in, head_grad, masked, seq_in, factors, others[-1]],
        name="prepare",
    )
    mixes, gateds, row_grads, fars = [], [], [], []
    for c in range(z.fronts):
        mix, gated, *row_grad = call(
            bind(channel_mix_kernel, z, c),
            [struct((z.front, z.width))] * 2 + block_outs(z, z.piece),
            [owns[c], gots[c], pads, upstream, seq_out],
            [pltpu.VMEM((z.seq, z.piece, z.width), BF16)],
            name="channel_mix",
        )
        mixes.append(mix)
        gateds.append(gated)
        row_grads.append(row_grad)
        fars.append(send_far(z, row_grad))
    joined_scratch = pltpu.VMEM((z.seq, z.group, z.width), BF16)
    mix0, mix1, *row_mix = call(
        bind(row_mix_kernel, z),
        [struct(chunk)] * 2 + block_outs(z, z.group),
        [turned] + mixes,
        [joined_scratch],
        name="row_mix",
    )
    mixes = [mix0, mix1]
    row_grads = exchange_blocks(z, row_grads, fars, row_mix[0])
    if z.direct:
        outs = [struct((z.group // 2, seq_in.shape[1]))] * 4
    else:
        outs = [struct(seq_in.shape, F32)]
    all_rows, *first_parts = call(
        bind(seq_grad_kernel, z, len(row_grads)),
        [struct(wide)] + outs,
        mixes + row_grads,
        [joined_scratch],
        name="seq_grad",
    )
    after = upstream
    if z.direct:
        keeps = call(bind(own_product_kernel, z), outs, mixes + [all_rows], name="own_product")
        core_sums = sum_cores(keeps, first_parts)
        after = core_sums[0]
    seq_part, gate = call(
        bind(seq_part_kernel, z),
        [struct(wide, F32)] * 2,
        [seq_in, all_rows] + mixes + [upstream, after],
        name="seq_part",
    )
    tokens_t, own_t, got_t = call(
        bind(turn_kernel, z),
        [struct((z.width, z.positions))] + [struct((2 * z.part, z.half))] * 2,
        [tokens] + owns + gots + [seq_part],
        name="turn",
    )
    spread = exchange_blocks(z, [row_mix], [send_far(z, row_mix)], tokens_t)
    mix_grad, own_grad, other_grad, spread = call(
        bind(mix_grad_kernel, z),
        [struct(wide), struct((z.half, 2 * z.part)), struct((z.half, 2 * z.part)), struct(wide)],
        [gate, seq_part, pads, seq_out] + spread,
        [joined_scratch],
        flops=MIX_FLOPS,
        name="mix_grad",
    )
    got_grad = swap(other_grad, "chan", 1)
    in_part, small = call(
        bind(out_grad_kernel, z),
        [struct((z.pack_in, PACK_LANES), F32), struct((z.pack_rows - z.pack_in, PACK_LANES))],
        [own_t, got_t, tokens_t, mix_grad, own_grad] + gateds + [spread],
        flops=OUT_FLOPS,
        name="out_grad",
    )
    pieces = z.seq if z.direct else 1

    x_part, token = call(
        bind(own_x_grad_kernel, z),
        [struct(wide, F32), struct((16, PACK_LANES), F32)],
        [in_mats, own_grad, small],
        flops=OWN_X_FLOPS,
        name="own_x_grad",
    )

    def pack_after(after):
        packs = call(
            bind(pack_kernel, z),
            [struct((z.pack_rows // pieces, PACK_LANES))] * pieces,
            [tokens_t, got_grad, in_part, small, token, after],
            [pltpu.VMEM((z.pack_rows, PACK_LANES), BF16)],
            name="pack",
        )
        x_grad, done = call(
            bind(x_grad_kernel, z),
            [struct(wide), struct((16, PACK_LANES))],
            [in_mats, x_part, got_grad, packs[0]],
            flops=X_FLOPS,
            name="x_grad",
        )
        return packs, x_grad, done

    outs = [
        struct(chan_in.shape, F32),
        struct((z.blocks, z.blocks, z.block), F32),
        struct(seq_out.shape, F32),
    ]
    if z.direct:
        x_grad, first_rows, in_sum, out_sum, second_sum = sum_factors(
            z, core_sums, pack_after, own_grad, small, outs
        )
    else:
        packs, x_grad, _ = pack_after(small)
        first_rows, in_sum, out_sum, second_sum = sum_factors_plain(z, *first_parts, *packs, outs)
    return (x_grad[None], in_sum, jnp.transpose(out_sum, (2, 0, 1)), first_rows, second_sum)


def solution(mesh):
    in_specs = (P("dp", "seq", "chan"), P(), P(), P(), P(), P("dp", "seq", "chan"), P("dp", "seq"))
    out_specs = (P("dp", "seq", "chan"), P(), P(), P("seq", None), P())
    return jax.shard_map(
        per_device, mesh=mesh, in_specs=in_specs, out_specs=out_specs, check_vma=False
    )
```
